32 devices in a mesh: group: 2 (over y), dom: 4 (over z), dp: 2 (over x), feat: 2 (over core).
Axes of the slice: x: 2, y: 2, z: 4, core: 2. Of those that a mesh axis runs over, the one named last changes fastest.
Arguments:
- node_latents: bfloat16 [4, 384, 512], P(('group', 'dp'), 'dom', 'feat'), parts along dimension 0, may hold values from -6 to 6
- edge_latents: bfloat16 [4, 3072, 512], P(('group', 'dp'), 'dom', 'feat'), parts along dimension 0, may hold values from -6 to 6
- grad_nodes: bfloat16 [4, 384, 512], P(('group', 'dp'), 'dom', 'feat'), parts along dimension 0, may hold values from -6 to 6
- grad_edges: bfloat16 [4, 3072, 512], P(('group', 'dp'), 'dom', 'feat'), parts along dimension 0, may hold values from -6 to 6
- edge_sender: int32 [3072], P('dom'), may hold values from 0 to 143, as said below
- edge_receiver: int32 [3072], P('dom'), may hold values from -1 to 95, as said below
- halo_rows: int32 [4, 4, 12], P('dom'), may hold values from 0 to 95
- w_edge_in: bfloat16 [1536, 512], P(None, 'feat'), may hold values from -0.15625 to 0.15625
- w_edge_out: bfloat16 [512, 512], P(None, 'feat'), may hold values from -1 to 1
- w_node_in: bfloat16 [1024, 512], P(None, 'feat'), may hold values from -0.1875 to 0.1875
- w_node_out: bfloat16 [512, 512], P(None, 'feat'), may hold values from -1 to 1
Outputs:
- d_nodes: bfloat16 [4, 384, 512], P(('group', 'dp'), 'dom', 'feat'), parts along dimension 0
- d_edges: bfloat16 [4, 3072, 512], P(('group', 'dp'), 'dom', 'feat'), parts along dimension 0
- dw_edge_in: float32 [3072, 512], P(('group', 'dp'), 'feat'), parts along dimension 0
- dw_edge_out: float32 [1024, 512], P(('group', 'dp'), 'feat'), parts along dimension 0
- dw_node_in: float32 [2048, 512], P(('group', 'dp'), 'feat'), parts along dimension 0
- dw_node_out: float32 [1024, 512], P(('group', 'dp'), 'feat'), parts along dimension 0
The draws below stay inside these ranges and needn't reach their ends.
There are 2 independent parts, one for each index of `group`. The reference program is written for one: setup_inputs(seed, part) draws one part's arguments, and reference() takes and returns one part's arrays. A program takes and returns all parts, laid end to end along the dimension named above; an argument that names none is the same for every part. Nothing has to cross between parts.
Inputs may be any that keep to these rules, and one draw needn't show every extreme that they name: `edge_receiver`: in each partition's 768 slots the live edges come first and each holds a receiver of that partition; every later slot holds -1. Each partition has at least max(96, 4) live slots, and in every draw some partition has all 768 live. `edge_sender`: A value t below 96 names node t of the slot's own partition; t = 96 + q * 12 + k names what partition q sends to the slot's partition in halo slot k, with q never the slot's own partition. Padding slots hold 0.
All inputs are finite; a program needn't handle non-finite values.
Results may differ from the reference program's by a relative error of at most 0.014.
Values may be sent and summed in bfloat16 or wider, within the bound.
A program may use at most 64 MiB of HBM per device.

```python
import math
import jax
import jax.numpy as jnp
from jax import lax

D = 512
HID = 512
NODE_DEV = 96
EDGE_DEV = 768
HALO = 12
NODES = 384
EDGES = 3072
SAMPLES = 2
N_DOM = 4


def edge_tables(key):
    keys = jax.random.split(key, 10)
    lowest = max(EDGE_DEV // 8, N_DOM)
    counts = jax.random.randint(keys[0], (N_DOM,), lowest, EDGE_DEV // 2 + 1)
    full_flag = jax.random.randint(keys[1], (N_DOM,), 0, 8) == 0
    chosen = jax.random.randint(keys[2], (), 0, N_DOM)
    full_flag = jnp.logical_or(full_flag, jnp.arange(N_DOM) == chosen)
    counts = jnp.where(full_flag, EDGE_DEV, counts)
    slot_index = jnp.arange(EDGE_DEV, dtype=jnp.int32)[None, :]
    part_index = jnp.arange(N_DOM, dtype=jnp.int32)[:, None]
    live_slot = slot_index < counts[:, None]
    is_local = jax.random.randint(keys[3], (N_DOM, EDGE_DEV), 0, 4) != 0
    local_index = jax.random.randint(keys[4], (N_DOM, EDGE_DEV), 0, NODE_DEV)
    near_table = jnp.array([1, 2, N_DOM - 1, N_DOM - 2], dtype=jnp.int32)
    near_pick = jax.random.randint(keys[8], (N_DOM, EDGE_DEV), 0, 4)
    near_step = jnp.sum(jnp.where(near_pick[:, :, None] == jnp.arange(4, dtype=jnp.int32)[None, None, :], near_table[None, None, :], 0), axis=2)
    far_step = jax.random.randint(keys[5], (N_DOM, EDGE_DEV), 1, N_DOM)
    use_near = jax.random.randint(keys[9], (N_DOM, EDGE_DEV), 0, 10) != 0
    peer_step = jnp.where(use_near, near_step, far_step)
    peer_part = (part_index + peer_step) % N_DOM
    halo_slot = jax.random.randint(keys[6], (N_DOM, EDGE_DEV), 0, HALO)
    forced = jnp.broadcast_to(slot_index < N_DOM, (N_DOM, EDGE_DEV))
    forced_peer = jnp.broadcast_to(slot_index % N_DOM, (N_DOM, EDGE_DEV))
    peer_part = jnp.where(forced, forced_peer, peer_part)
    halo_slot = jnp.where(forced, HALO - 1 - part_index % HALO, halo_slot)
    is_local = jnp.where(forced, forced_peer == part_index, is_local)
    sender = jnp.where(is_local, local_index, NODE_DEV + peer_part * HALO + halo_slot)
    receiver = jax.random.randint(keys[7], (N_DOM, EDGE_DEV), 0, NODE_DEV)
    sender = jnp.where(live_slot, sender, 0).astype(jnp.int32)
    receiver = jnp.where(live_slot, receiver, -1).astype(jnp.int32)
    return (sender.reshape(-1), receiver.reshape(-1))


def column_scaled(key, row_count, column_count, lowest, highest):
    keys = jax.random.split(key, 3)
    entries = jnp.clip(jax.random.normal(keys[0], (row_count, column_count), jnp.float32), -6.0, 6.0)
    column_scale = jnp.exp(jax.random.uniform(keys[2], (1, column_count), jnp.float32, math.log(lowest), math.log(highest)))
    values = entries * column_scale * row_count ** (-0.5)
    return jnp.clip(values, -1.0, 1.0).astype(jnp.bfloat16)


def draw_edge_sender(key, part):
    tables = edge_tables(key)
    return tables[0]


def draw_edge_receiver(key, part):
    tables = edge_tables(key)
    return tables[1]


def draw_w_edge_out(key, part):
    key = jax.random.fold_in(key, 11)
    return column_scaled(key, HID, D, 0.3, 3.0)


def draw_w_node_out(key, part):
    key = jax.random.fold_in(key, 12)
    return column_scaled(key, HID, D, 0.3, 3.0)


def plant(values, own_key, low, top_value):
    spot = [jax.random.randint(jax.random.fold_in(own_key, axis), (), 0, length) for axis, length in enumerate(values.shape)]
    longest = values.shape.index(max(values.shape))
    neighbour = spot[:longest] + [(spot[longest] + 1) % values.shape[longest]] + spot[longest + 1:]
    return values.at[tuple(spot)].set(low).at[tuple(neighbour)].set(top_value)


def block_levels(rng, dims, cuts, low, largest):
    def one(dim, blocks):
        draws = jax.random.uniform(jax.random.fold_in(jax.random.fold_in(rng, 6), dim), (blocks,), jnp.float32, low / len(cuts), largest / len(cuts))
        return jnp.repeat(jnp.exp(draws), dims[dim] // blocks).reshape((-1,) + (1,) * (len(dims) - dim - 1))

    level = one(*cuts[0])
    for cut in cuts[1:]:
        level = level * one(*cut)
    return level


def normal_values(own_key, shape, spread, bound, cuts=(), held_as=jnp.bfloat16):
    values = spread * jax.random.normal(own_key, shape, jnp.float32)
    if cuts:
        values = values * block_levels(own_key, shape, cuts, -0.22, 0.18)
    return jnp.clip(values, -bound, bound).astype(held_as)


def setup_inputs(seed: int = 0, part: int = 0) -> dict:
    key_of = jax.random.split(jax.random.key(seed), 12)
    part_keys = jax.random.split(jax.random.fold_in(key_of[11], part), 12)
    node_latents = normal_values(part_keys[0], (SAMPLES, NODES, D), 1.0, 6.0, ((0, 2), (1, 4), (2, 2)))
    edge_latents = normal_values(part_keys[1], (SAMPLES, EDGES, D), 1.0, 6.0, ((0, 2), (1, 4), (2, 2)))
    grad_nodes = normal_values(part_keys[2], (SAMPLES, NODES, D), 1.0, 6.0, ((0, 2), (1, 4), (2, 2)))
    grad_edges = normal_values(part_keys[3], (SAMPLES, EDGES, D), 1.0, 6.0, ((0, 2), (1, 4), (2, 2)))
    edge_sender = draw_edge_sender(jax.random.fold_in(key_of[11], 71), part)
    edge_receiver = draw_edge_receiver(jax.random.fold_in(key_of[11], 71), part)
    halo_rows = plant(jax.random.randint(key_of[6], (N_DOM, N_DOM, HALO), 0, NODE_DEV), jax.random.fold_in(key_of[6], 1), 0, NODE_DEV - 1).astype(jnp.int32)
    w_edge_in = normal_values(key_of[7], (3 * D, HID), (3 * D) ** -0.5, 0.15625, ((1, 2),))
    w_edge_out = draw_w_edge_out(jax.random.fold_in(key_of[11], 71), part)
    w_node_in = normal_values(key_of[9], (2 * D, HID), (2 * D) ** -0.5, 0.1875, ((1, 2),))
    w_node_out = draw_w_node_out(jax.random.fold_in(key_of[11], 71), part)
    return {"node_latents": node_latents, "edge_latents": edge_latents, "grad_nodes": grad_nodes, "grad_edges": grad_edges, "edge_sender": edge_sender, "edge_receiver": edge_receiver, "halo_rows": halo_rows, "w_edge_in": w_edge_in, "w_edge_out": w_edge_out, "w_node_in": w_node_in, "w_node_out": w_node_out}


EPSILON = 1e-05

def silu_slope(preact):
    sigmoid = jax.nn.sigmoid(preact)
    return sigmoid * (1.0 + preact * (1.0 - sigmoid))

def rounded(values):
    return lax.optimization_barrier(values.astype(jnp.bfloat16))

def product(first, second):
    return jnp.dot(first, second, preferred_element_type=jnp.float32)

def product_tn(first, second):
    return lax.dot_general(first, second, (((0,), (0,)), ((), ())), preferred_element_type=jnp.float32)

def product_nt(first, second):
    return lax.dot_general(first, second, (((1,), (1,)), ((), ())), preferred_element_type=jnp.float32)

def norm_forward(values):
    row_mean = lax.optimization_barrier(jnp.mean(values, axis=-1, keepdims=True))
    centered = values - row_mean
    inverse = lax.rsqrt(lax.optimization_barrier(jnp.mean(centered * centered, axis=-1, keepdims=True)) + EPSILON)
    return (centered * inverse, inverse)

def norm_backward(upstream, normed, inverse):
    grad_mean = lax.optimization_barrier(jnp.mean(upstream, axis=-1, keepdims=True))
    cross_mean = lax.optimization_barrier(jnp.mean(upstream * normed, axis=-1, keepdims=True))
    return inverse * (upstream - grad_mean - normed * cross_mean)

def reference(node_latents, edge_latents, grad_nodes, grad_edges, edge_sender, edge_receiver, halo_rows, w_edge_in, w_edge_out, w_node_in, w_node_out):
    part_of = (jnp.arange(EDGES, dtype=jnp.int32) // EDGE_DEV).astype(jnp.int32)
    remote = jnp.maximum(edge_sender - NODE_DEV, 0).astype(jnp.int32)
    peer_part = (remote // HALO).astype(jnp.int32)
    peer_slot = (remote % HALO).astype(jnp.int32)
    remote_node = peer_part * NODE_DEV + halo_rows[peer_part, part_of, peer_slot]
    send_node = jnp.where(edge_sender < NODE_DEV, part_of * NODE_DEV + edge_sender, remote_node).astype(jnp.int32)
    live_rows = (edge_receiver >= 0)[:, None]
    recv_node = jnp.where(edge_receiver >= 0, part_of * NODE_DEV + edge_receiver, 0).astype(jnp.int32)

    def one_sample(inputs):
        node_rows, edge_rows, node_cot, edge_cot = inputs
        edge_input = jnp.concatenate([edge_rows, node_rows[send_node], node_rows[recv_node]], axis=1)
        edge_pre = product(edge_input, w_edge_in)
        edge_act = rounded(jax.nn.silu(edge_pre))
        edge_normed, edge_inverse = norm_forward(product(edge_act, w_edge_out))
        message = rounded(jnp.where(live_rows, edge_normed, 0.0))
        summed = rounded(jax.ops.segment_sum(message.astype(jnp.float32), recv_node, num_segments=NODES))
        node_input = jnp.concatenate([node_rows, summed], axis=1)
        node_pre = product(node_input, w_node_in)
        node_act = rounded(jax.nn.silu(node_pre))
        node_normed, node_inverse = norm_forward(product(node_act, w_node_out))
        node_out_grad = rounded(norm_backward(node_cot.astype(jnp.float32), node_normed, node_inverse))
        dw_node_out = product_tn(node_act, node_out_grad)
        node_pre_grad = rounded(product_nt(node_out_grad, w_node_out) * silu_slope(node_pre))
        dw_node_in = product_tn(node_input, node_pre_grad)
        node_input_grad = product_nt(node_pre_grad, w_node_in)
        summed_grad = rounded(node_input_grad[:, D:])
        message_grad = jnp.where(live_rows, edge_cot.astype(jnp.float32) + summed_grad[recv_node].astype(jnp.float32), 0.0)
        edge_out_grad = rounded(norm_backward(message_grad, edge_normed, edge_inverse))
        dw_edge_out = product_tn(edge_act, edge_out_grad)
        edge_pre_grad = rounded(product_nt(edge_out_grad, w_edge_out) * silu_slope(edge_pre))
        dw_edge_in = product_tn(edge_input, edge_pre_grad)
        edge_input_grad = rounded(product_nt(edge_pre_grad, w_edge_in)).astype(jnp.float32)
        edge_grad = (edge_cot.astype(jnp.float32) + edge_input_grad[:, :D]).astype(jnp.bfloat16)
        node_terms = node_input_grad[:, :D]
        node_terms = node_terms + jax.ops.segment_sum(edge_input_grad[:, D:2 * D], send_node, num_segments=NODES)
        node_terms = node_terms + jax.ops.segment_sum(edge_input_grad[:, 2 * D:], recv_node, num_segments=NODES)
        return (node_terms.astype(jnp.bfloat16), edge_grad, dw_edge_in, dw_edge_out, dw_node_in, dw_node_out)
    results = lax.map(one_sample, (node_latents, edge_latents, grad_nodes, grad_edges))
    edge_factor = 1.0 / math.sqrt(SAMPLES * EDGES)
    node_factor = 1.0 / math.sqrt(SAMPLES * NODES)
    return (results[0], results[1], lax.optimization_barrier(jnp.sum(results[2], axis=0)) * edge_factor, lax.optimization_barrier(jnp.sum(results[3], axis=0)) * edge_factor, lax.optimization_barrier(jnp.sum(results[4], axis=0)) * node_factor, lax.optimization_barrier(jnp.sum(results[5], axis=0)) * node_factor)
```

```python
import functools
import math

import jax
import jax.numpy as jnp
from jax import lax
from jax.experimental import pallas as pl
from jax.experimental.pallas import tpu as pltpu
from jax.sharding import PartitionSpec as P

EPSILON = 1e-05
F32 = jnp.float32
BF16 = jnp.bfloat16
CHUNK = 128
SLOT = 16


def product(first, second):
    return jnp.dot(first, second, preferred_element_type=F32)


def product_tn(first, second):
    return lax.dot_general(first, second, (((0,), (0,)), ((), ())), preferred_element_type=F32)


def product_nt(first, second):
    return lax.dot_general(first, second, (((1,), (1,)), ((), ())), preferred_element_type=F32)


def silu_and_slope(v):
    s = 1.0 / (1.0 + jnp.exp(-v))
    return v * s, s * (1.0 + v * (1.0 - s))


def round_up(value, step):
    return -(-value // step) * step


def norm_forward(lo, hi, width):
    mean = (jnp.sum(lo, axis=1, keepdims=True) + jnp.sum(hi, axis=1, keepdims=True)) / width
    lo, hi = lo - mean, hi - mean
    spread = (
        jnp.sum(lo * lo, axis=1, keepdims=True) + jnp.sum(hi * hi, axis=1, keepdims=True)
    ) / width
    inv = lax.rsqrt(spread + EPSILON)
    return lo * inv, hi * inv, inv


def norm_backward(glo, ghi, nlo, nhi, inv, width):
    gm = (jnp.sum(glo, axis=1, keepdims=True) + jnp.sum(ghi, axis=1, keepdims=True)) / width
    cm = (
        jnp.sum(glo * nlo, axis=1, keepdims=True) + jnp.sum(ghi * nhi, axis=1, keepdims=True)
    ) / width
    return inv * (glo - gm - nlo * cm), inv * (ghi - gm - nhi * cm)


def kernel(
    cfg,
    nodes, edges, gnodes, gedges, w_ei, w_eo, w_ni, w_no, snd, rcv, halo,
    o_nodes, o_edges, res,
    table, gn, e, ge, wei, weo, wni, wno,
    hout, hot_s, hot_r, x, pre, act, normed, msg_part, msg_other,
    n_in, n_act, n_og, n_pg, sgrad, eog, epg, dbuf, np_send, np_recv, tg, hback,
    fsend, frecv, own, dw, xrecv, share, up, child,
    loc, fs, fr, hs, hr, ts, tr, xs, xr, us, ur, ds, dr,
):
    nD, nS, N, R, K = cfg["nD"], cfg["nS"], cfg["N"], cfg["R"], cfg["HALO"]
    H = 256
    D = 2 * H
    Tp = table.shape[1]
    HP = halo.shape[1]
    d, s, f = lax.axis_index("dom"), lax.axis_index("dp"), lax.axis_index("feat")
    g = 1 - f
    pending = []

    def remote(src, dst, ss, rs, dev):
        cp = pltpu.make_async_remote_copy(
            src_ref=src, dst_ref=dst, send_sem=ss, recv_sem=rs,
            device_id=dev, device_id_type=pl.DeviceIdType.MESH,
        )
        return cp

    def send(src, dst, ss, rs, dev):
        cp = remote(src, dst, ss, rs, dev)
        cp.start()
        pending.append(cp)

    partner = {"feat": g}

    mine = pl.ds(pl.multiple_of(f * R, R), R)
    theirs = pl.ds(pl.multiple_of(g * R, R), R)
    locals_ = [
        (nodes.at[0], table.at[f, pl.ds(0, N)]),
        (edges.at[0, mine], e.at[f]),
        (w_ei, wei.at[f]),
        (w_eo, weo.at[f]),
        (gnodes.at[0], gn.at[f]),
        (w_ni, wni.at[f]),
        (w_no, wno.at[f]),
        (gedges.at[0, mine], ge.at[f]),
    ]
    lcp = []
    for i, (a, b) in enumerate(locals_):
        c = pltpu.make_async_copy(a, b, loc.at[i])
        c.start()
        lcp.append(c)

    bar = pltpu.get_barrier_semaphore()

    def greet(dev):
        pl.semaphore_signal(bar, inc=1, device_id=dev, device_id_type=pl.DeviceIdType.MESH)

    greet(partner)
    for o in range(1, nD):
        q = lax.rem(d + o, nD)
        for h in range(2):
            greet({"dom": q, "feat": h})
    for o in range(1, nS):
        greet({"dp": lax.rem(s + o, nS)})

    for h in range(2):
        table[h, pl.ds(pl.multiple_of(N + d * SLOT, SLOT), SLOT), :] = jnp.zeros((SLOT, H), BF16)
        hback[h, pl.ds(pl.multiple_of(d * SLOT, SLOT), SLOT), :] = jnp.zeros((SLOT, H), BF16)
        if Tp > N + nD * SLOT:
            table[h, N + nD * SLOT :, :] = jnp.zeros((Tp - N - nD * SLOT, H), BF16)
        if HP > nD * SLOT:
            hback[h, nD * SLOT :, :] = jnp.zeros((HP - nD * SLOT, H), BF16)
    cols = pl.ds(pl.multiple_of(f * R, 128), R)
    t = snd[:, cols]
    far = jnp.maximum(t - N, 0)
    q_of = lax.shift_right_logical(far * cfg["MUL"], 19)
    t = jnp.where(t < N, t, t + q_of * (SLOT - K))
    hot_s[...] = jnp.where(
        lax.broadcasted_iota(jnp.int32, (Tp, R), 0) == t, 1.0, 0.0
    ).astype(BF16)
    hot_r[...] = jnp.where(
        lax.broadcasted_iota(jnp.int32, (N, R), 0) == rcv[:, cols], 1.0, 0.0
    ).astype(BF16)
    hot_h = jnp.where(
        lax.broadcasted_iota(jnp.int32, (N, HP), 0) == halo[...], 1.0, 0.0
    ).astype(BF16)
    lcp[0].wait()
    hout[...] = product_tn(hot_h, table[f, :N, :]).astype(BF16)

    pl.semaphore_wait(bar, 1 + 2 * (nD - 1) + (nS - 1))

    for o in range(1, nD):
        q = lax.rem(d + o, nD)
        for h in range(2):
            send(
                hout.at[pl.ds(pl.multiple_of(q * SLOT, SLOT), SLOT)],
                table.at[f, pl.ds(pl.multiple_of(N + d * SLOT, SLOT), SLOT)],
                hs.at[q, h], hr.at[d, f], {"dom": q, "feat": h},
            )
    rem_src = [
        nodes.at[0], edges.at[0, theirs], w_ei, w_eo, gnodes.at[0], w_ni, w_no,
        gedges.at[0, theirs],
    ]
    for i, src in enumerate(rem_src):
        send(src, locals_[i][1], fs.at[i], fr.at[i], partner)
    arrive = [
        table.at[g, pl.ds(0, N)], e.at[g], wei.at[g], weo.at[g], gn.at[g], wni.at[g], wno.at[g],
        ge.at[g],
    ]

    def got(i):
        if i:
            lcp[i].wait()
        remote(arrive[i], arrive[i], fs.at[i], fr.at[i], partner).wait_recv()

    got(0)
    got(1)
    for h in range(2):
        x[:, h * H : (h + 1) * H] = e[h]
        x[:, 2 * D + h * H : 2 * D + (h + 1) * H] = product_tn(
            hot_r[...], table[h, :N, :]
        ).astype(BF16)
    for o in range(1, nD):
        q = lax.rem(d + nD - o, nD)
        for h in range(2):
            dst = table.at[h, pl.ds(pl.multiple_of(N + q * SLOT, SLOT), SLOT)]
            remote(dst, dst, hs.at[q, h], hr.at[q, h], partner).wait_recv()
    for h in range(2):
        x[:, D + h * H : D + (h + 1) * H] = product_tn(hot_s[...], table[h]).astype(BF16)
    got(2)
    for h in range(2):
        v = product(x[...], wei[h])
        pre[h] = v
        a, _ = silu_and_slope(v)
        act[:, h * H : (h + 1) * H] = a.astype(BF16)
    got(3)
    lo, hi, inv = norm_forward(product(act[...], weo[0]), product(act[...], weo[1]), D)
    normed[0], normed[1] = lo, hi
    e_inv = inv
    msg_part[:, :H] = product(hot_r[...], lo.astype(BF16))
    msg_part[:, H:] = product(hot_r[...], hi.astype(BF16))
    send(msg_part, msg_other, fs.at[8], fr.at[8], partner)
    got(4)
    got(5)
    n_in[:, :H] = table[0, :N, :]
    n_in[:, H:D] = table[1, :N, :]
    first = [product(n_in[:, :D], wni[h, :D, :]) for h in range(2)]
    remote(msg_other, msg_other, fs.at[8], fr.at[8], partner).wait_recv()
    n_in[:, D:] = (msg_part[...] + msg_other[...]).astype(BF16)
    slopes = []
    for h in range(2):
        v = first[h] + product(n_in[:, D:], wni[h, D:, :])
        a, b = silu_and_slope(v)
        slopes.append(b)
        n_act[:, h * H : (h + 1) * H] = a.astype(BF16)
    got(6)
    lo, hi, inv = norm_forward(product(n_act[...], wno[0]), product(n_act[...], wno[1]), D)
    lo, hi = norm_backward(gn[0].astype(F32), gn[1].astype(F32), lo, hi, inv, D)
    n_og[0], n_og[1] = lo.astype(BF16), hi.astype(BF16)
    v = product_nt(n_og[0], wno[0]) + product_nt(n_og[1], wno[1])
    n_pg[0] = (v[:, :H] * slopes[0]).astype(BF16)
    n_pg[1] = (v[:, H:] * slopes[1]).astype(BF16)
    v = product_nt(n_pg[0], wni[0, D:, :]) + product_nt(n_pg[1], wni[1, D:, :])
    sgrad[...] = v.astype(BF16)

    sizes = [D // nS // CHUNK, 2 * D // nS // CHUNK, D // nS // CHUNK, 3 * D // nS // CHUNK]
    bases = [0, sizes[0], sizes[0] + sizes[1], sizes[0] + sizes[1] + sizes[2]]
    nch = sum(sizes)
    efirst = bases[2]

    def block(ref, i, sp):
        w = sizes[i] * CHUNK
        return ref[:, pl.ds(pl.multiple_of(sp * w, CHUNK), w)]

    def ship(i, sp):
        for j in range(sizes[i]):
            c = bases[i] + j
            send(dw.at[sp, c], xrecv.at[s, c], xs.at[sp, c], xr.at[s, c], {"dp": sp})

    for i, lhs, rhs in ((0, n_act, n_og), (1, n_in, n_pg)):
        for o in list(range(1, nS)) + [0]:
            sp = lax.rem(s + o, nS)
            v = product_tn(block(lhs, i, sp), rhs[f]) * cfg["node_factor"]
            dw[sp, bases[i] : bases[i] + sizes[i]] = v.reshape(sizes[i], CHUNK, H).astype(BF16)
            if o:
                ship(i, sp)

    root = nD // 2 - 1
    left = d < root
    side = jnp.where(left, 0, 1)
    is_root = d == root
    leaf = jnp.logical_or(d == 0, d == nD - 1)
    toward = jnp.where(left, d + 1, jnp.maximum(d - 1, 0))
    away = jnp.where(left, jnp.maximum(d - 1, 0), jnp.minimum(d + 1, nD - 1))

    def up_copy(c):
        return remote(up.at[c], child.at[side, c], us.at[c], ur.at[side, c], {"dom": toward})

    def child_wait(k, c):
        remote(up.at[c], child.at[k, c], us.at[c], ur.at[k, c], {"dom": toward}).wait_recv()

    def down_copy(c, k, dev):
        return remote(res.at[c], res.at[c], ds.at[k, c], dr.at[c], {"dom": dev})

    def stage_a(c):
        total = dw[s, c].astype(F32)
        for o in range(1, nS):
            sp = lax.rem(s + o, nS)
            remote(dw.at[sp, c], xrecv.at[sp, c], xs.at[sp, c], xr.at[sp, c], {"dp": sp}).wait_recv()
            total += xrecv[sp, c].astype(F32)

        @pl.when(leaf)
        def _():
            up[c] = total.astype(BF16)
            up_copy(c).start()

        @pl.when(jnp.logical_not(leaf))
        def _():
            share[c] = total

    def stage_b(c):
        @pl.when(jnp.logical_not(jnp.logical_or(leaf, is_root)))
        def _():
            child_wait(side, c)
            up[c] = (share[c] + child[side, c].astype(F32)).astype(BF16)
            up_copy(c).start()

    def stage_r(c):
        @pl.when(is_root)
        def _():
            child_wait(0, c)
            child_wait(1, c)
            res[c] = (share[c] + child[0, c].astype(F32) + child[1, c].astype(F32)).astype(BF16)
            down_copy(c, 0, root - 1).start()
            down_copy(c, 1, root + 1).start()

    def stage_d(c):
        @pl.when(jnp.logical_not(is_root))
        def _():
            down_copy(c, 0, away).wait_recv()

            @pl.when(jnp.logical_not(leaf))
            def _():
                down_copy(c, 0, away).start()

    def step(tt):
        for fn, lag in ((stage_a, 0), (stage_b, 1), (stage_r, 2), (stage_d, 4)):
            c = tt - lag
            if 0 <= c < nch:
                fn(c)

    clock = [0]

    def advance(limit):
        while clock[0] < limit:
            step(clock[0])
            clock[0] += 1

    got(7)
    live = product_tn(hot_r[...], jnp.ones((N, 128), BF16))[:, :1]
    glo = live * (ge[0].astype(F32) + product_tn(hot_r[...], sgrad[:, :H]))
    ghi = live * (ge[1].astype(F32) + product_tn(hot_r[...], sgrad[:, H:]))
    lo, hi = norm_backward(glo, ghi, normed[0], normed[1], e_inv, D)
    eog[0], eog[1] = lo.astype(BF16), hi.astype(BF16)
    v = product_nt(eog[0], weo[0]) + product_nt(eog[1], weo[1])
    for h in range(2):
        _, b = silu_and_slope(pre[h])
        epg[h] = (v[:, h * H : (h + 1) * H] * b).astype(BF16)

    order = list(range(1, nS)) + [0]
    edge_items = ((2, act, eog), (3, x, epg))
    for i, lhs, rhs in edge_items:
        lo_c = bases[i] - efirst
        for o in order:
            sp = lax.rem(s + o, nS)
            v = product_tn(block(lhs, i, sp), rhs[g]) * cfg["edge_factor"]
            fsend[sp, lo_c : lo_c + sizes[i]] = v.reshape(sizes[i], CHUNK, H).astype(BF16)
            part = pl.ds(lo_c, sizes[i])
            k = 11 + (i - 2) * nS
            send(fsend.at[sp, part], frecv.at[sp, part], fs.at[k + sp], fr.at[k + sp], partner)
    for i, lhs, rhs in edge_items:
        lo_c = bases[i] - efirst
        part = pl.ds(lo_c, sizes[i])
        k = 11 + (i - 2) * nS
        for o in order:
            sp = lax.rem(s + o, nS)
            v = product_tn(block(lhs, i, sp), rhs[f]) * cfg["edge_factor"]
            dst = frecv.at[sp, part]
            remote(dst, dst, fs.at[k + sp], fr.at[k + sp], partner).wait_recv()
            v = v.reshape(sizes[i], CHUNK, H) + frecv[sp, lo_c : lo_c + sizes[i]].astype(F32)
            dw[sp, bases[i] : bases[i] + sizes[i]] = v.astype(BF16)
            if o:
                ship(i, sp)
    advance(efirst)

    for hh in range(2):
        h = g if hh == 0 else f
        rows = pl.ds(pl.multiple_of(h * H, H), H)
        v = product_nt(epg[0], wei[0, rows, :]) + product_nt(epg[1], wei[1, rows, :])
        out = (ge[h].astype(F32) + v.astype(BF16).astype(F32)).astype(BF16)
        if hh == 0:
            dbuf[...] = out
            send(dbuf, o_edges.at[mine], fs.at[9], fr.at[9], partner)
        else:
            o_edges[mine, :] = out
    for hh in range(2):
        h = g if hh == 0 else f
        rows_s = pl.ds(pl.multiple_of(D + h * H, H), H)
        rows_r = pl.ds(pl.multiple_of(2 * D + h * H, H), H)
        vs = (product_nt(epg[0], wei[0, rows_s, :]) + product_nt(epg[1], wei[1, rows_s, :])).astype(BF16)
        vr = (product_nt(epg[0], wei[0, rows_r, :]) + product_nt(epg[1], wei[1, rows_r, :])).astype(BF16)
        tgv = product(hot_s[...], vs)
        tg[h] = tgv[N : N + nD * SLOT].astype(BF16)
        for o in range(1, nD):
            q = lax.rem(d + o, nD)
            send(
                tg.at[h, pl.ds(pl.multiple_of(q * SLOT, SLOT), SLOT)],
                hback.at[f, pl.ds(pl.multiple_of(d * SLOT, SLOT), SLOT)],
                ts.at[q, h], tr.at[d, f], {"dom": q, "feat": h},
            )
        nv = tgv[:N] + product(hot_r[...], vr)
        if hh == 0:
            np_send[...] = nv
            send(np_send, np_recv, fs.at[10], fr.at[10], partner)
    rows = pl.ds(pl.multiple_of(f * H, H), H)
    nv += product_nt(n_pg[0], wni[0, rows, :]) + product_nt(n_pg[1], wni[1, rows, :])
    remote(np_recv, np_recv, fs.at[10], fr.at[10], partner).wait_recv()
    nv += np_recv[...]
    for o in range(1, nD):
        q = lax.rem(d + nD - o, nD)
        for h in range(2):
            dst = hback.at[h, pl.ds(pl.multiple_of(q * SLOT, SLOT), SLOT)]
            remote(dst, dst, ts.at[q, h], tr.at[q, h], partner).wait_recv()
    hot_h = jnp.where(
        lax.broadcasted_iota(jnp.int32, (N, HP), 0) == halo[...], 1.0, 0.0
    ).astype(BF16)
    nv += product(hot_h, hback[0]) + product(hot_h, hback[1])
    o_nodes[...] = nv.astype(BF16)
    advance(nch + 5)
    dst = o_edges.at[theirs]
    remote(dst, dst, fs.at[9], fr.at[9], partner).wait_recv()

    for cp in pending:
        cp.wait_send()
    for c in range(nch):
        @pl.when(jnp.logical_not(is_root))
        def _():
            up_copy(c).wait_send()

        @pl.when(jnp.logical_or(is_root, jnp.logical_not(leaf)))
        def _():
            down_copy(c, 0, away).wait_send()

        @pl.when(is_root)
        def _():
            down_copy(c, 1, away).wait_send()


def shards(node_latents, edge_latents, grad_nodes, grad_edges, edge_sender, edge_receiver,
           halo_rows, w_ei, w_eo, w_ni, w_no):
    nD, nS = lax.axis_size("dom"), lax.axis_size("dp")
    N, EC = node_latents.shape[1], edge_latents.shape[1]
    H = node_latents.shape[2]
    D = 2 * H
    R = EC // 2
    K = halo_rows.shape[2]
    HP = round_up(nD * SLOT, 128)
    Tp = round_up(N + nD * SLOT, 128)
    mul = -(-(1 << 19) // K)
    assert all((v * mul) >> 19 == v // K for v in range(nD * K))
    halo = jnp.pad(halo_rows[0], ((0, 0), (0, SLOT - K)), constant_values=-1).reshape(1, -1)
    if HP > nD * SLOT:
        halo = jnp.pad(halo, ((0, 0), (0, HP - nD * SLOT)), constant_values=-1)
    nch = 7 * D // nS // CHUNK
    nce = 4 * D // nS // CHUNK
    cfg = dict(
        nD=nD, nS=nS, N=N, R=R, HALO=K, MUL=mul,
        edge_factor=1.0 / math.sqrt(nS * EC * nD), node_factor=1.0 / math.sqrt(nS * N * nD),
    )
    vm = lambda shape, dt=BF16: pltpu.VMEM(shape, dt)
    sem = lambda *shape: pltpu.SemaphoreType.DMA(shape)
    any_, vmem = pl.BlockSpec(memory_space=pl.ANY), pl.BlockSpec(memory_space=pltpu.VMEM)
    scratch = [
        vm((2, Tp, H)), vm((2, N, H)), vm((2, R, H)), vm((2, R, H)),
        vm((2, 3 * D, H)), vm((2, D, H)), vm((2, 2 * D, H)), vm((2, D, H)),
        vm((HP, H)), vm((Tp, R)), vm((N, R)), vm((R, 3 * D)), vm((2, R, H), F32), vm((R, D)),
        vm((2, R, H), F32), vm((N, D), F32), vm((N, D), F32),
        vm((N, 2 * D)), vm((N, D)), vm((2, N, H)), vm((2, N, H)), vm((N, D)),
        vm((2, R, H)), vm((2, R, H)), vm((R, H)), vm((N, H), F32), vm((N, H), F32),
        vm((2, nD * SLOT, H)), vm((2, HP, H)),
        vm((nS, nce, CHUNK, H)), vm((nS, nce, CHUNK, H)), vm((8, 128), F32),
        vm((nS, nch, CHUNK, H)), vm((nS, nch, CHUNK, H)), vm((nch, CHUNK, H), F32),
        vm((nch, CHUNK, H)), vm((2, nch, CHUNK, H)),
        sem(8), sem(11 + 2 * nS), sem(11 + 2 * nS), sem(nD, 2), sem(nD, 2), sem(nD, 2), sem(nD, 2),
        sem(nS, nch), sem(nS, nch), sem(nch), sem(2, nch), sem(2, nch), sem(nch),
    ]
    d_nodes, d_edges, dw = pl.pallas_call(
        functools.partial(kernel, cfg),
        out_shape=(
            jax.ShapeDtypeStruct((N, H), BF16),
            jax.ShapeDtypeStruct((EC, H), BF16),
            jax.ShapeDtypeStruct((nch, CHUNK, H), BF16),
        ),
        in_specs=[any_] * 8 + [vmem] * 3,
        out_specs=(vmem, vmem, vmem),
        scratch_shapes=scratch,
        compiler_params=pltpu.CompilerParams(
            collective_id=0, has_side_effects=True, vmem_limit_bytes=50 * 1024 * 1024
        ),
        cost_estimate=pl.CostEstimate(
            flops=4_000_000_000, bytes_accessed=8_000_000, transcendentals=1_000_000
        ),
    )(node_latents, edge_latents, grad_nodes, grad_edges, w_ei, w_eo, w_ni, w_no,
      edge_sender.reshape(1, -1), edge_receiver.reshape(1, -1), halo)
    dw = dw.reshape(nch * CHUNK, H)
    a, b = D // nS, 2 * D // nS
    g_no, g_ni = dw[:a], dw[a : a + b]
    g_eo, g_ei = dw[a + b : 2 * a + b], dw[2 * a + b :]
    return (d_nodes[None], d_edges[None], g_ei.astype(F32), g_eo.astype(F32), g_ni.astype(F32),
            g_no.astype(F32))


def solution(mesh):
    whole = P(("group", "dp"), "dom", "feat")
    weight = P(None, "feat")
    share = P(("group", "dp"), "feat")
    return jax.shard_map(
        shards,
        mesh=mesh,
        in_specs=(whole,) * 4 + (P("dom"), P("dom"), P("dom", None, None)) + (weight,) * 4,
        out_specs=(whole, whole, share, share, share, share),
        check_vma=False,
    )
```

```python
import functools
import math

import jax
import jax.numpy as jnp
from jax import lax
from jax.experimental import pallas as pl
from jax.experimental.pallas import tpu as pltpu
from jax.sharding import PartitionSpec as P

EPSILON = 1e-05
F32 = jnp.float32
BF16 = jnp.bfloat16
CHUNK = 128
SLOT = 16
LAG_B, LAG_R, LAG_D = 3, 6, 10


def product(first, second):
    return jnp.dot(first, second, preferred_element_type=F32)


def product_tn(first, second):
    return lax.dot_general(first, second, (((0,), (0,)), ((), ())), preferred_element_type=F32)


def product_nt(first, second):
    return lax.dot_general(first, second, (((1,), (1,)), ((), ())), preferred_element_type=F32)


def silu_and_slope(v):
    s = 1.0 / (1.0 + jnp.exp(-v))
    return v * s, s * (1.0 + v * (1.0 - s))


def round_up(value, step):
    return -(-value // step) * step


def norm_forward(lo, hi, width):
    mean = (jnp.sum(lo, axis=1, keepdims=True) + jnp.sum(hi, axis=1, keepdims=True)) / width
    lo, hi = lo - mean, hi - mean
    spread = (
        jnp.sum(lo * lo, axis=1, keepdims=True) + jnp.sum(hi * hi, axis=1, keepdims=True)
    ) / width
    inv = lax.rsqrt(spread + EPSILON)
    return lo * inv, hi * inv, inv


def norm_backward(glo, ghi, nlo, nhi, inv, width):
    gm = (jnp.sum(glo, axis=1, keepdims=True) + jnp.sum(ghi, axis=1, keepdims=True)) / width
    cm = (
        jnp.sum(glo * nlo, axis=1, keepdims=True) + jnp.sum(ghi * nhi, axis=1, keepdims=True)
    ) / width
    return inv * (glo - gm - nlo * cm), inv * (ghi - gm - nhi * cm)


def kernel(
    cfg,
    nodes, edges, gnodes, gedges, w_ei, w_eo, w_ni, w_no, ints,
    o_nodes, o_edges, res,
    table, gn, e, ge, wei, weo, wni, wno,
    hout, hot_s, hot_r, x, pre, act, normed, msg_part, msg_other,
    n_in, n_act, n_og, n_pg, sgrad, eog, epg, dbuf, np_send, np_recv, tg, hback,
    fsend, frecv, own, dw, xrecv, share, up, child,
    loc, fs, fr, hs, hr, ts, tr, xs, xr, us, ur, ds, dr,
):
    nD, nS, N, R, K = cfg["nD"], cfg["nS"], cfg["N"], cfg["R"], cfg["HALO"]
    H = 256
    D = 2 * H
    Tp = table.shape[1]
    HP = hout.shape[0]
    d, s, f = lax.axis_index("dom"), lax.axis_index("dp"), lax.axis_index("feat")
    g = 1 - f
    pending = []

    def remote(src, dst, ss, rs, dev):
        cp = pltpu.make_async_remote_copy(
            src_ref=src, dst_ref=dst, send_sem=ss, recv_sem=rs,
            device_id=dev, device_id_type=pl.DeviceIdType.MESH,
        )
        return cp

    def send(src, dst, ss, rs, dev):
        cp = remote(src, dst, ss, rs, dev)
        cp.start()
        pending.append(cp)

    partner = {"feat": g}

    mine = pl.ds(pl.multiple_of(f * R, R), R)
    theirs = pl.ds(pl.multiple_of(g * R, R), R)
    locals_ = [
        (nodes.at[0], table.at[f, pl.ds(0, N)]),
        (edges.at[0, mine], e.at[f]),
        (w_ei, wei.at[f]),
        (w_eo, weo.at[f]),
        (gnodes.at[0], gn.at[f]),
        (w_ni, wni.at[f]),
        (w_no, wno.at[f]),
        (gedges.at[0, mine], ge.at[f]),
    ]
    lcp = []
    for i, (a, b) in enumerate(locals_):
        c = pltpu.make_async_copy(a, b, loc.at[i])
        c.start()
        lcp.append(c)

    bar = pltpu.get_barrier_semaphore()

    def greet(dev):
        pl.semaphore_signal(bar, inc=1, device_id=dev, device_id_type=pl.DeviceIdType.MESH)

    greet(partner)
    for o in range(1, nD):
        q = lax.rem(d + o, nD)
        for h in range(2):
            greet({"dom": q, "feat": h})
    for o in range(1, nS):
        greet({"dp": lax.rem(s + o, nS)})

    for h in range(2):
        table[h, pl.ds(pl.multiple_of(N + d * SLOT, SLOT), SLOT), :] = jnp.zeros((SLOT, H), BF16)
        hback[h, pl.ds(pl.multiple_of(d * SLOT, SLOT), SLOT), :] = jnp.zeros((SLOT, H), BF16)
        if Tp > N + nD * SLOT:
            table[h, N + nD * SLOT :, :] = jnp.zeros((Tp - N - nD * SLOT, H), BF16)
        if HP > nD * SLOT:
            hback[h, nD * SLOT :, :] = jnp.zeros((HP - nD * SLOT, H), BF16)
    cols = pl.ds(pl.multiple_of(f * R, 128), R)
    t = ints[:, cols]
    far = jnp.maximum(t - N, 0)
    q_of = lax.shift_right_logical(far * cfg["MUL"], 19)
    t = jnp.where(t < N, t, t + q_of * (SLOT - K))
    hot_s[...] = jnp.where(
        lax.broadcasted_iota(jnp.int32, (Tp, R), 0) == t, 1.0, 0.0
    ).astype(BF16)
    hot_r[...] = jnp.where(
        lax.broadcasted_iota(jnp.int32, (N, R), 0) == ints[:, pl.ds(pl.multiple_of(2 * R + f * R, 128), R)], 1.0, 0.0
    ).astype(BF16)
    hot_h = jnp.where(
        lax.broadcasted_iota(jnp.int32, (N, HP), 0) == ints[:, 4 * R :], 1.0, 0.0
    ).astype(BF16)
    lcp[0].wait()
    hout[...] = product_tn(hot_h, table[f, :N, :]).astype(BF16)

    pl.semaphore_wait(bar, 1 + 2 * (nD - 1) + (nS - 1))

    for o in range(1, nD):
        q = lax.rem(d + o, nD)
        for h in range(2):
            send(
                hout.at[pl.ds(pl.multiple_of(q * SLOT, SLOT), SLOT)],
                table.at[f, pl.ds(pl.multiple_of(N + d * SLOT, SLOT), SLOT)],
                hs.at[q, h], hr.at[d, f], {"dom": q, "feat": h},
            )
    rem_src = [
        nodes.at[0], edges.at[0, theirs], w_ei, w_eo, gnodes.at[0], w_ni, w_no,
        gedges.at[0, theirs],
    ]
    for i, src in enumerate(rem_src):
        send(src, locals_[i][1], fs.at[i], fr.at[i], partner)
    arrive = [
        table.at[g, pl.ds(0, N)], e.at[g], wei.at[g], weo.at[g], gn.at[g], wni.at[g], wno.at[g],
        ge.at[g],
    ]

    def got(i):
        if i:
            lcp[i].wait()
        remote(arrive[i], arrive[i], fs.at[i], fr.at[i], partner).wait_recv()

    got(0)
    got(1)
    for h in range(2):
        x[:, h * H : (h + 1) * H] = e[h]
        x[:, 2 * D + h * H : 2 * D + (h + 1) * H] = product_tn(
            hot_r[...], table[h, :N, :]
        ).astype(BF16)
    for o in range(1, nD):
        q = lax.rem(d + nD - o, nD)
        for h in range(2):
            dst = table.at[h, pl.ds(pl.multiple_of(N + q * SLOT, SLOT), SLOT)]
            remote(dst, dst, hs.at[q, h], hr.at[q, h], partner).wait_recv()
    for h in range(2):
        x[:, D + h * H : D + (h + 1) * H] = product_tn(hot_s[...], table[h]).astype(BF16)
    got(2)
    for h in range(2):
        v = product(x[...], wei[h])
        pre[h] = v
        a, _ = silu_and_slope(v)
        act[:, h * H : (h + 1) * H] = a.astype(BF16)
    got(3)
    lo, hi, inv = norm_forward(product(act[...], weo[0]), product(act[...], weo[1]), D)
    normed[0], normed[1] = lo, hi
    e_inv = inv
    msg_part[:, :H] = product(hot_r[...], lo.astype(BF16))
    msg_part[:, H:] = product(hot_r[...], hi.astype(BF16))
    send(msg_part, msg_other, fs.at[8], fr.at[8], partner)
    got(4)
    got(5)
    n_in[:, :H] = table[0, :N, :]
    n_in[:, H:D] = table[1, :N, :]
    first = [product(n_in[:, :D], wni[h, :D, :]) for h in range(2)]
    remote(msg_other, msg_other, fs.at[8], fr.at[8], partner).wait_recv()
    n_in[:, D:] = (msg_part[...] + msg_other[...]).astype(BF16)
    slopes = []
    for h in range(2):
        v = first[h] + product(n_in[:, D:], wni[h, D:, :])
        a, b = silu_and_slope(v)
        slopes.append(b)
        n_act[:, h * H : (h + 1) * H] = a.astype(BF16)
    got(6)
    lo, hi, inv = norm_forward(product(n_act[...], wno[0]), product(n_act[...], wno[1]), D)
    lo, hi = norm_backward(gn[0].astype(F32), gn[1].astype(F32), lo, hi, inv, D)
    n_og[0], n_og[1] = lo.astype(BF16), hi.astype(BF16)
    v = product_nt(n_og[0], wno[0]) + product_nt(n_og[1], wno[1])
    n_pg[0] = (v[:, :H] * slopes[0]).astype(BF16)
    n_pg[1] = (v[:, H:] * slopes[1]).astype(BF16)
    v = product_nt(n_pg[0], wni[0, D:, :]) + product_nt(n_pg[1], wni[1, D:, :])
    sgrad[...] = v.astype(BF16)

    sizes = [D // nS // CHUNK, 2 * D // nS // CHUNK, D // nS // CHUNK, 3 * D // nS // CHUNK]
    bases = [0, sizes[0], sizes[0] + sizes[1], sizes[0] + sizes[1] + sizes[2]]
    nch = sum(sizes)
    efirst = bases[2]

    def block(ref, i, sp):
        w = sizes[i] * CHUNK
        return ref[:, pl.ds(pl.multiple_of(sp * w, CHUNK), w)]

    def ship(i, sp):
        for j in range(sizes[i]):
            c = bases[i] + j
            send(dw.at[sp, c], xrecv.at[s, c], xs.at[sp, c], xr.at[s, c], {"dp": sp})

    for i, lhs, rhs in ((0, n_act, n_og), (1, n_in, n_pg)):
        for o in list(range(1, nS)) + [0]:
            sp = lax.rem(s + o, nS)
            v = product_tn(block(lhs, i, sp), rhs[f]) * cfg["node_factor"]
            dw[sp, bases[i] : bases[i] + sizes[i]] = v.reshape(sizes[i], CHUNK, H).astype(BF16)
            if o:
                ship(i, sp)

    root = nD // 2 - 1
    left = d < root
    side = jnp.where(left, 0, 1)
    is_root = d == root
    leaf = jnp.logical_or(d == 0, d == nD - 1)
    toward = jnp.where(left, d + 1, jnp.maximum(d - 1, 0))
    away = jnp.where(left, jnp.maximum(d - 1, 0), jnp.minimum(d + 1, nD - 1))

    def up_copy(c):
        return remote(up.at[c], child.at[side, c], us.at[c], ur.at[side, c], {"dom": toward})

    def child_wait(k, c):
        remote(up.at[c], child.at[k, c], us.at[c], ur.at[k, c], {"dom": toward}).wait_recv()

    def down_copy(c, k, dev):
        return remote(res.at[c], res.at[c], ds.at[k, c], dr.at[c], {"dom": dev})

    def stage_a(c):
        total = dw[s, c].astype(F32)
        for o in range(1, nS):
            sp = lax.rem(s + o, nS)
            remote(dw.at[sp, c], xrecv.at[sp, c], xs.at[sp, c], xr.at[sp, c], {"dp": sp}).wait_recv()
            total += xrecv[sp, c].astype(F32)

        @pl.when(leaf)
        def _():
            up[c] = total.astype(BF16)
            up_copy(c).start()

        @pl.when(jnp.logical_not(leaf))
        def _():
            share[c] = total

    def stage_b(c):
        @pl.when(jnp.logical_not(jnp.logical_or(leaf, is_root)))
        def _():
            child_wait(side, c)
            up[c] = (share[c] + child[side, c].astype(F32)).astype(BF16)
            up_copy(c).start()

    def stage_r(c):
        @pl.when(is_root)
        def _():
            child_wait(0, c)
            child_wait(1, c)
            res[c] = (share[c] + child[0, c].astype(F32) + child[1, c].astype(F32)).astype(BF16)
            down_copy(c, 0, root - 1).start()
            down_copy(c, 1, root + 1).start()

    def stage_d(c):
        @pl.when(jnp.logical_not(is_root))
        def _():
            down_copy(c, 0, away).wait_recv()

            @pl.when(jnp.logical_not(leaf))
            def _():
                down_copy(c, 0, away).start()

    def step(tt):
        for fn, lag in ((stage_a, 0), (stage_b, LAG_B), (stage_r, LAG_R), (stage_d, LAG_D)):
            c = tt - lag
            if 0 <= c < nch:
                fn(c)

    clock = [0]

    def advance(limit):
        while clock[0] < limit:
            step(clock[0])
            clock[0] += 1

    got(7)
    live = product_tn(hot_r[...], jnp.ones((N, 128), BF16))[:, :1]
    glo = live * (ge[0].astype(F32) + product_tn(hot_r[...], sgrad[:, :H]))
    ghi = live * (ge[1].astype(F32) + product_tn(hot_r[...], sgrad[:, H:]))
    lo, hi = norm_backward(glo, ghi, normed[0], normed[1], e_inv, D)
    eog[0], eog[1] = lo.astype(BF16), hi.astype(BF16)
    order = list(range(1, nS)) + [0]

    def across(i, lhs, rhs):
        lo_c = bases[i] - efirst
        part = pl.ds(lo_c, sizes[i])
        k = 11 + (i - 2) * nS
        for o in order:
            sp = lax.rem(s + o, nS)
            v = product_tn(block(lhs, i, sp), rhs[g]) * cfg["edge_factor"]
            fsend[sp, lo_c : lo_c + sizes[i]] = v.reshape(sizes[i], CHUNK, H).astype(BF16)
            send(fsend.at[sp, part], frecv.at[sp, part], fs.at[k + sp], fr.at[k + sp], partner)

    def combine(i, lhs, rhs):
        lo_c = bases[i] - efirst
        part = pl.ds(lo_c, sizes[i])
        k = 11 + (i - 2) * nS
        for o in order:
            sp = lax.rem(s + o, nS)
            v = product_tn(block(lhs, i, sp), rhs[f]) * cfg["edge_factor"]
            dst = frecv.at[sp, part]
            remote(dst, dst, fs.at[k + sp], fr.at[k + sp], partner).wait_recv()
            v = v.reshape(sizes[i], CHUNK, H) + frecv[sp, lo_c : lo_c + sizes[i]].astype(F32)
            dw[sp, bases[i] : bases[i] + sizes[i]] = v.astype(BF16)
            if o:
                ship(i, sp)

    across(2, act, eog)
    v = product_nt(eog[0], weo[0]) + product_nt(eog[1], weo[1])
    for h in range(2):
        _, b = silu_and_slope(pre[h])
        epg[h] = (v[:, h * H : (h + 1) * H] * b).astype(BF16)
    combine(2, act, eog)
    advance(3)
    across(3, x, epg)
    advance(6)
    combine(3, x, epg)
    advance(efirst + 2)

    for hh in range(2):
        h = g if hh == 0 else f
        rows = pl.ds(pl.multiple_of(h * H, H), H)
        v = product_nt(epg[0], wei[0, rows, :]) + product_nt(epg[1], wei[1, rows, :])
        out = (ge[h].astype(F32) + v.astype(BF16).astype(F32)).astype(BF16)
        if hh == 0:
            dbuf[...] = out
            send(dbuf, o_edges.at[mine], fs.at[9], fr.at[9], partner)
        else:
            o_edges[mine, :] = out
    advance(efirst + 4)
    for hh in range(2):
        h = g if hh == 0 else f
        rows_s = pl.ds(pl.multiple_of(D + h * H, H), H)
        rows_r = pl.ds(pl.multiple_of(2 * D + h * H, H), H)
        vs = (product_nt(epg[0], wei[0, rows_s, :]) + product_nt(epg[1], wei[1, rows_s, :])).astype(BF16)
        vr = (product_nt(epg[0], wei[0, rows_r, :]) + product_nt(epg[1], wei[1, rows_r, :])).astype(BF16)
        tgv = product(hot_s[...], vs)
        tg[h] = tgv[N : N + nD * SLOT].astype(BF16)
        for o in range(1, nD):
            q = lax.rem(d + o, nD)
            send(
                tg.at[h, pl.ds(pl.multiple_of(q * SLOT, SLOT), SLOT)],
                hback.at[f, pl.ds(pl.multiple_of(d * SLOT, SLOT), SLOT)],
                ts.at[q, h], tr.at[d, f], {"dom": q, "feat": h},
            )
        nv = tgv[:N] + product(hot_r[...], vr)
        advance(efirst + 6 + 2 * hh)
        if hh == 0:
            np_send[...] = nv
            send(np_send, np_recv, fs.at[10], fr.at[10], partner)
    rows = pl.ds(pl.multiple_of(f * H, H), H)
    nv += product_nt(n_pg[0], wni[0, rows, :]) + product_nt(n_pg[1], wni[1, rows, :])
    remote(np_recv, np_recv, fs.at[10], fr.at[10], partner).wait_recv()
    nv += np_recv[...]
    for o in range(1, nD):
        q = lax.rem(d + nD - o, nD)
        for h in range(2):
            dst = hback.at[h, pl.ds(pl.multiple_of(q * SLOT, SLOT), SLOT)]
            remote(dst, dst, ts.at[q, h], tr.at[q, h], partner).wait_recv()
    hot_h = jnp.where(
        lax.broadcasted_iota(jnp.int32, (N, HP), 0) == ints[:, 4 * R :], 1.0, 0.0
    ).astype(BF16)
    nv += product(hot_h, hback[0]) + product(hot_h, hback[1])
    o_nodes[...] = nv.astype(BF16)
    advance(nch + LAG_D)
    dst = o_edges.at[theirs]
    remote(dst, dst, fs.at[9], fr.at[9], partner).wait_recv()

    for cp in pending:
        cp.wait_send()
    for c in range(nch):
        @pl.when(jnp.logical_not(is_root))
        def _():
            up_copy(c).wait_send()

        @pl.when(jnp.logical_or(is_root, jnp.logical_not(leaf)))
        def _():
            down_copy(c, 0, away).wait_send()

        @pl.when(is_root)
        def _():
            down_copy(c, 1, away).wait_send()


def spread(rows, nodes, edges, dw, o_nodes, o_edges, *outs):
    o_nodes[0] = nodes[...]
    o_edges[0] = edges[...]
    at = 0
    for r, out in zip(rows, outs):
        out[...] = dw[at : at + r].astype(F32).reshape(r * CHUNK, dw.shape[2])
        at += r


def shards(node_latents, edge_latents, grad_nodes, grad_edges, edge_sender, edge_receiver,
           halo_rows, w_ei, w_eo, w_ni, w_no):
    nD, nS = lax.axis_size("dom"), lax.axis_size("dp")
    N, EC = node_latents.shape[1], edge_latents.shape[1]
    H = node_latents.shape[2]
    D = 2 * H
    R = EC // 2
    K = halo_rows.shape[2]
    HP = round_up(nD * SLOT, 128)
    Tp = round_up(N + nD * SLOT, 128)
    mul = -(-(1 << 19) // K)
    assert all((v * mul) >> 19 == v // K for v in range(nD * K))
    halo = jnp.pad(
        halo_rows[0], ((0, HP // SLOT - nD), (0, SLOT - K)), constant_values=-1
    ).reshape(-1)
    ints = jnp.concatenate([edge_sender, edge_receiver, halo]).reshape(1, -1)
    nch = 7 * D // nS // CHUNK
    nce = 4 * D // nS // CHUNK
    cfg = dict(
        nD=nD, nS=nS, N=N, R=R, HALO=K, MUL=mul,
        edge_factor=1.0 / math.sqrt(nS * EC * nD), node_factor=1.0 / math.sqrt(nS * N * nD),
    )
    vm = lambda shape, dt=BF16: pltpu.VMEM(shape, dt)
    sem = lambda *shape: pltpu.SemaphoreType.DMA(shape)
    any_, vmem = pl.BlockSpec(memory_space=pl.ANY), pl.BlockSpec(memory_space=pltpu.VMEM)
    scratch = [
        vm((2, Tp, H)), vm((2, N, H)), vm((2, R, H)), vm((2, R, H)),
        vm((2, 3 * D, H)), vm((2, D, H)), vm((2, 2 * D, H)), vm((2, D, H)),
        vm((HP, H)), vm((Tp, R)), vm((N, R)), vm((R, 3 * D)), vm((2, R, H), F32), vm((R, D)),
        vm((2, R, H), F32), vm((N, D), F32), vm((N, D), F32),
        vm((N, 2 * D)), vm((N, D)), vm((2, N, H)), vm((2, N, H)), vm((N, D)),
        vm((2, R, H)), vm((2, R, H)), vm((R, H)), vm((N, H), F32), vm((N, H), F32),
        vm((2, nD * SLOT, H)), vm((2, HP, H)),
        vm((nS, nce, CHUNK, H)), vm((nS, nce, CHUNK, H)), vm((8, 128), F32),
        vm((nS, nch, CHUNK, H)), vm((nS, nch, CHUNK, H)), vm((nch, CHUNK, H), F32),
        vm((nch, CHUNK, H)), vm((2, nch, CHUNK, H)),
        sem(8), sem(11 + 2 * nS), sem(11 + 2 * nS), sem(nD, 2), sem(nD, 2), sem(nD, 2), sem(nD, 2),
        sem(nS, nch), sem(nS, nch), sem(nch), sem(2, nch), sem(2, nch), sem(nch),
    ]
    d_nodes, d_edges, dw = pl.pallas_call(
        functools.partial(kernel, cfg),
        out_shape=(
            jax.ShapeDtypeStruct((N, H), BF16),
            jax.ShapeDtypeStruct((EC, H), BF16),
            jax.ShapeDtypeStruct((nch, CHUNK, H), BF16),
        ),
        in_specs=[any_] * 8 + [vmem],
        out_specs=(vmem, vmem, vmem),
        scratch_shapes=scratch,
        compiler_params=pltpu.CompilerParams(
            collective_id=0, has_side_effects=True, vmem_limit_bytes=62 * 1024 * 1024
        ),
        cost_estimate=pl.CostEstimate(
            flops=4_000_000_000, bytes_accessed=8_000_000, transcendentals=1_000_000
        ),
    )(node_latents, edge_latents, grad_nodes, grad_edges, w_ei, w_eo, w_ni, w_no,
      ints)
    rows = (D // nS // CHUNK, 2 * D // nS // CHUNK, D // nS // CHUNK, 3 * D // nS // CHUNK)
    out = lambda r: jax.ShapeDtypeStruct((r * CHUNK, H), F32)
    d_nodes, d_edges, g_no, g_ni, g_eo, g_ei = pl.pallas_call(
        functools.partial(spread, rows),
        out_shape=(
            jax.ShapeDtypeStruct((1, N, H), BF16), jax.ShapeDtypeStruct((1, EC, H), BF16),
            out(rows[0]), out(rows[1]), out(rows[2]), out(rows[3]),
        ),
        in_specs=[vmem] * 3,
        out_specs=(vmem,) * 6,
        compiler_params=pltpu.CompilerParams(vmem_limit_bytes=62 * 1024 * 1024),
        cost_estimate=pl.CostEstimate(flops=500_000, bytes_accessed=4_000_000, transcendentals=0),
    )(d_nodes, d_edges, dw)
    return d_nodes, d_edges, g_ei, g_eo, g_ni, g_no


def solution(mesh):
    whole = P(("group", "dp"), "dom", "feat")
    weight = P(None, "feat")
    share = P(("group", "dp"), "feat")
    return jax.shard_map(
        shards,
        mesh=mesh,
        in_specs=(whole,) * 4 + (P("dom"), P("dom"), P("dom", None, None)) + (weight,) * 4,
        out_specs=(whole, whole, share, share, share, share),
        check_vma=False,
    )
```

```python
import functools
import math

import jax
import jax.numpy as jnp
from jax import lax
from jax.experimental import pallas as pl
from jax.experimental.pallas import tpu as pltpu
from jax.sharding import PartitionSpec as P

EPSILON = 1e-05
F32 = jnp.float32
BF16 = jnp.bfloat16
CHUNK = 128
SLOT = 16
LAG_B, LAG_R, LAG_D = 3, 6, 9


def product(first, second):
    return jnp.dot(first, second, preferred_element_type=F32)


def product_tn(first, second):
    return lax.dot_general(first, second, (((0,), (0,)), ((), ())), preferred_element_type=F32)


def product_nt(first, second):
    return lax.dot_general(first, second, (((1,), (1,)), ((), ())), preferred_element_type=F32)


def silu_and_slope(v):
    s = 1.0 / (1.0 + jnp.exp(-v))
    return v * s, s * (1.0 + v * (1.0 - s))


def round_up(value, step):
    return -(-value // step) * step


def norm_forward(lo, hi, width):
    mean = (jnp.sum(lo, axis=1, keepdims=True) + jnp.sum(hi, axis=1, keepdims=True)) / width
    lo, hi = lo - mean, hi - mean
    spread = (
        jnp.sum(lo * lo, axis=1, keepdims=True) + jnp.sum(hi * hi, axis=1, keepdims=True)
    ) / width
    inv = lax.rsqrt(spread + EPSILON)
    return lo * inv, hi * inv, inv


def norm_backward(glo, ghi, nlo, nhi, inv, width):
    gm = (jnp.sum(glo, axis=1, keepdims=True) + jnp.sum(ghi, axis=1, keepdims=True)) / width
    cm = (
        jnp.sum(glo * nlo, axis=1, keepdims=True) + jnp.sum(ghi * nhi, axis=1, keepdims=True)
    ) / width
    return inv * (glo - gm - nlo * cm), inv * (ghi - gm - nhi * cm)


def kernel(
    cfg,
    nodes, edges, gnodes, gedges, w_ei, w_eo, w_ni, w_no, ints,
    o_nodes, o_edges, res,
    table, gn, e, ge, wei, weo, wni, wno,
    hout, hot_s, hot_r, x, pre, act, normed, msg_part, msg_other,
    n_in, n_act, n_og, n_pg, sgrad, eog, epg, dbuf, np_send, np_recv, tg, hback,
    fsend, frecv, own, dw, xrecv, share, up, child,
    loc, fs, fr, hs, hr, ts, tr, xs, xr, us, ur, ds, dr,
):
    nD, nS, N, R, K = cfg["nD"], cfg["nS"], cfg["N"], cfg["R"], cfg["HALO"]
    H = 256
    D = 2 * H
    Tp = table.shape[1]
    HP = hout.shape[0]
    d, s, f = lax.axis_index("dom"), lax.axis_index("dp"), lax.axis_index("feat")
    g = 1 - f
    pending = []

    def remote(src, dst, ss, rs, dev):
        cp = pltpu.make_async_remote_copy(
            src_ref=src, dst_ref=dst, send_sem=ss, recv_sem=rs,
            device_id=dev, device_id_type=pl.DeviceIdType.MESH,
        )
        return cp

    def send(src, dst, ss, rs, dev):
        cp = remote(src, dst, ss, rs, dev)
        cp.start()
        pending.append(cp)

    partner = {"feat": g}

    mine = pl.ds(pl.multiple_of(f * R, R), R)
    theirs = pl.ds(pl.multiple_of(g * R, R), R)
    locals_ = [
        (nodes.at[0], table.at[f, pl.ds(0, N)]),
        (edges.at[0, mine], e.at[f]),
        (w_ei, wei.at[f]),
        (w_eo, weo.at[f]),
        (gnodes.at[0], gn.at[f]),
        (w_ni, wni.at[f]),
        (w_no, wno.at[f]),
        (gedges.at[0, mine], ge.at[f]),
    ]
    lcp = []
    for i, (a, b) in enumerate(locals_):
        c = pltpu.make_async_copy(a, b, loc.at[i])
        c.start()
        lcp.append(c)

    bar = pltpu.get_barrier_semaphore()

    def greet(dev):
        pl.semaphore_signal(bar, inc=1, device_id=dev, device_id_type=pl.DeviceIdType.MESH)

    greet(partner)
    for o in range(1, nD):
        q = lax.rem(d + o, nD)
        for h in range(2):
            greet({"dom": q, "feat": h})
    for o in range(1, nS):
        greet({"dp": lax.rem(s + o, nS)})

    for h in range(2):
        table[h, pl.ds(pl.multiple_of(N + d * SLOT, SLOT), SLOT), :] = jnp.zeros((SLOT, H), BF16)
        hback[h, pl.ds(pl.multiple_of(d * SLOT, SLOT), SLOT), :] = jnp.zeros((SLOT, H), BF16)
        if Tp > N + nD * SLOT:
            table[h, N + nD * SLOT :, :] = jnp.zeros((Tp - N - nD * SLOT, H), BF16)
        if HP > nD * SLOT:
            hback[h, nD * SLOT :, :] = jnp.zeros((HP - nD * SLOT, H), BF16)
    cols = pl.ds(pl.multiple_of(f * R, 128), R)
    t = ints[:, cols]
    far = jnp.maximum(t - N, 0)
    q_of = lax.shift_right_logical(far * cfg["MUL"], 19)
    t = jnp.where(t < N, t, t + q_of * (SLOT - K))
    hot_s[...] = jnp.where(
        lax.broadcasted_iota(jnp.int32, (Tp, R), 0) == t, 1.0, 0.0
    ).astype(BF16)
    hot_r[...] = jnp.where(
        lax.broadcasted_iota(jnp.int32, (N, R), 0) == ints[:, pl.ds(pl.multiple_of(2 * R + f * R, 128), R)], 1.0, 0.0
    ).astype(BF16)
    hot_h = jnp.where(
        lax.broadcasted_iota(jnp.int32, (N, HP), 0) == ints[:, 4 * R :], 1.0, 0.0
    ).astype(BF16)
    lcp[0].wait()
    hout[...] = product_tn(hot_h, table[f, :N, :]).astype(BF16)

    pl.semaphore_wait(bar, 1 + 2 * (nD - 1) + (nS - 1))

    for o in range(1, nD):
        q = lax.rem(d + o, nD)
        for h in range(2):
            send(
                hout.at[pl.ds(pl.multiple_of(q * SLOT, SLOT), SLOT)],
                table.at[f, pl.ds(pl.multiple_of(N + d * SLOT, SLOT), SLOT)],
                hs.at[q, h], hr.at[d, f], {"dom": q, "feat": h},
            )
    rem_src = [
        nodes.at[0], edges.at[0, theirs], w_ei, w_eo, gnodes.at[0], w_ni, w_no,
        gedges.at[0, theirs],
    ]
    for i, src in enumerate(rem_src):
        send(src, locals_[i][1], fs.at[i], fr.at[i], partner)
    arrive = [
        table.at[g, pl.ds(0, N)], e.at[g], wei.at[g], weo.at[g], gn.at[g], wni.at[g], wno.at[g],
        ge.at[g],
    ]

    def got(i):
        if i:
            lcp[i].wait()
        remote(arrive[i], arrive[i], fs.at[i], fr.at[i], partner).wait_recv()

    got(0)
    got(1)
    for h in range(2):
        x[:, h * H : (h + 1) * H] = e[h]
        x[:, 2 * D + h * H : 2 * D + (h + 1) * H] = product_tn(
            hot_r[...], table[h, :N, :]
        ).astype(BF16)
    for o in range(1, nD):
        q = lax.rem(d + nD - o, nD)
        for h in range(2):
            dst = table.at[h, pl.ds(pl.multiple_of(N + q * SLOT, SLOT), SLOT)]
            remote(dst, dst, hs.at[q, h], hr.at[q, h], partner).wait_recv()
    for h in range(2):
        x[:, D + h * H : D + (h + 1) * H] = product_tn(hot_s[...], table[h]).astype(BF16)
    got(2)
    for h in range(2):
        v = product(x[...], wei[h])
        pre[h] = v
        a, _ = silu_and_slope(v)
        act[:, h * H : (h + 1) * H] = a.astype(BF16)
    got(3)
    lo, hi, inv = norm_forward(product(act[...], weo[0]), product(act[...], weo[1]), D)
    normed[0], normed[1] = lo, hi
    e_inv = inv
    msg_part[:, :H] = product(hot_r[...], lo.astype(BF16))
    msg_part[:, H:] = product(hot_r[...], hi.astype(BF16))
    send(msg_part, msg_other, fs.at[8], fr.at[8], partner)
    got(4)
    got(5)
    n_in[:, :H] = table[0, :N, :]
    n_in[:, H:D] = table[1, :N, :]
    first = [product(n_in[:, :D], wni[h, :D, :]) for h in range(2)]
    remote(msg_other, msg_other, fs.at[8], fr.at[8], partner).wait_recv()
    n_in[:, D:] = (msg_part[...] + msg_other[...]).astype(BF16)
    slopes = []
    for h in range(2):
        v = first[h] + product(n_in[:, D:], wni[h, D:, :])
        a, b = silu_and_slope(v)
        slopes.append(b)
        n_act[:, h * H : (h + 1) * H] = a.astype(BF16)
    got(6)
    lo, hi, inv = norm_forward(product(n_act[...], wno[0]), product(n_act[...], wno[1]), D)
    lo, hi = norm_backward(gn[0].astype(F32), gn[1].astype(F32), lo, hi, inv, D)
    n_og[0], n_og[1] = lo.astype(BF16), hi.astype(BF16)
    v = product_nt(n_og[0], wno[0]) + product_nt(n_og[1], wno[1])
    n_pg[0] = (v[:, :H] * slopes[0]).astype(BF16)
    n_pg[1] = (v[:, H:] * slopes[1]).astype(BF16)
    v = product_nt(n_pg[0], wni[0, D:, :]) + product_nt(n_pg[1], wni[1, D:, :])
    sgrad[...] = v.astype(BF16)

    sizes = [D // nS // CHUNK, 2 * D // nS // CHUNK, D // nS // CHUNK, 3 * D // nS // CHUNK]
    bases = [0, sizes[0], sizes[0] + sizes[1], sizes[0] + sizes[1] + sizes[2]]
    nch = sum(sizes)
    efirst = bases[2]

    def block(ref, i, sp):
        w = sizes[i] * CHUNK
        return ref[:, pl.ds(pl.multiple_of(sp * w, CHUNK), w)]

    def ship(i, sp):
        for j in range(sizes[i]):
            c = bases[i] + j
            send(dw.at[sp, c], xrecv.at[s, c], xs.at[sp, c], xr.at[s, c], {"dp": sp})

    for i, lhs, rhs in ((0, n_act, n_og), (1, n_in, n_pg)):
        for o in list(range(1, nS)) + [0]:
            sp = lax.rem(s + o, nS)
            v = product_tn(block(lhs, i, sp), rhs[f]) * cfg["node_factor"]
            dw[sp, bases[i] : bases[i] + sizes[i]] = v.reshape(sizes[i], CHUNK, H).astype(BF16)
            if o:
                ship(i, sp)

    root = nD // 2 - 1
    left = d < root
    side = jnp.where(left, 0, 1)
    is_root = d == root
    leaf = jnp.logical_or(d == 0, d == nD - 1)
    toward = jnp.where(left, d + 1, jnp.maximum(d - 1, 0))
    away = jnp.where(left, jnp.maximum(d - 1, 0), jnp.minimum(d + 1, nD - 1))

    def up_copy(c):
        return remote(up.at[c], child.at[side, c], us.at[c], ur.at[side, c], {"dom": toward})

    def child_wait(k, c):
        remote(up.at[c], child.at[k, c], us.at[c], ur.at[k, c], {"dom": toward}).wait_recv()

    def down_copy(c, k, dev):
        return remote(res.at[c], res.at[c], ds.at[k, c], dr.at[c], {"dom": dev})

    def stage_a(c):
        total = dw[s, c].astype(F32)
        for o in range(1, nS):
            sp = lax.rem(s + o, nS)
            remote(dw.at[sp, c], xrecv.at[sp, c], xs.at[sp, c], xr.at[sp, c], {"dp": sp}).wait_recv()
            total += xrecv[sp, c].astype(F32)

        @pl.when(leaf)
        def _():
            up[c] = total.astype(BF16)
            up_copy(c).start()

        @pl.when(jnp.logical_not(leaf))
        def _():
            share[c] = total

    def stage_b(c):
        @pl.when(jnp.logical_not(jnp.logical_or(leaf, is_root)))
        def _():
            child_wait(side, c)
            up[c] = (share[c] + child[side, c].astype(F32)).astype(BF16)
            up_copy(c).start()

    def stage_r(c):
        @pl.when(is_root)
        def _():
            child_wait(0, c)
            child_wait(1, c)
            res[c] = (share[c] + child[0, c].astype(F32) + child[1, c].astype(F32)).astype(BF16)
            down_copy(c, 0, root - 1).start()
            down_copy(c, 1, root + 1).start()

    def stage_d(c):
        @pl.when(jnp.logical_not(is_root))
        def _():
            down_copy(c, 0, away).wait_recv()

            @pl.when(jnp.logical_not(leaf))
            def _():
                down_copy(c, 0, away).start()

    def step(tt):
        for fn, lag in ((stage_a, 0), (stage_b, LAG_B), (stage_r, LAG_R), (stage_d, LAG_D)):
            c = tt - lag
            if 0 <= c < nch:
                fn(c)

    clock = [0]

    def advance(limit):
        while clock[0] < limit:
            step(clock[0])
            clock[0] += 1

    got(7)
    live = product_tn(hot_r[...], jnp.ones((N, 128), BF16))[:, :1]
    glo = live * (ge[0].astype(F32) + product_tn(hot_r[...], sgrad[:, :H]))
    ghi = live * (ge[1].astype(F32) + product_tn(hot_r[...], sgrad[:, H:]))
    lo, hi = norm_backward(glo, ghi, normed[0], normed[1], e_inv, D)
    eog[0], eog[1] = lo.astype(BF16), hi.astype(BF16)
    order = list(range(1, nS)) + [0]

    def across(i, lhs, rhs):
        lo_c = bases[i] - efirst
        part = pl.ds(lo_c, sizes[i])
        k = 11 + (i - 2) * nS
        for o in order:
            sp = lax.rem(s + o, nS)
            v = product_tn(block(lhs, i, sp), rhs[g]) * cfg["edge_factor"]
            fsend[sp, lo_c : lo_c + sizes[i]] = v.reshape(sizes[i], CHUNK, H).astype(BF16)
            send(fsend.at[sp, part], frecv.at[sp, part], fs.at[k + sp], fr.at[k + sp], partner)

    def combine(i, lhs, rhs):
        lo_c = bases[i] - efirst
        part = pl.ds(lo_c, sizes[i])
        k = 11 + (i - 2) * nS
        for o in order:
            sp = lax.rem(s + o, nS)
            v = product_tn(block(lhs, i, sp), rhs[f]) * cfg["edge_factor"]
            dst = frecv.at[sp, part]
            remote(dst, dst, fs.at[k + sp], fr.at[k + sp], partner).wait_recv()
            v = v.reshape(sizes[i], CHUNK, H) + frecv[sp, lo_c : lo_c + sizes[i]].astype(F32)
            dw[sp, bases[i] : bases[i] + sizes[i]] = v.astype(BF16)
            if o:
                ship(i, sp)

    across(2, act, eog)
    v = product_nt(eog[0], weo[0]) + product_nt(eog[1], weo[1])
    for h in range(2):
        _, b = silu_and_slope(pre[h])
        epg[h] = (v[:, h * H : (h + 1) * H] * b).astype(BF16)
    combine(2, act, eog)
    advance(3)
    across(3, x, epg)
    advance(6)
    combine(3, x, epg)
    advance(efirst + 2)

    for hh in range(2):
        h = g if hh == 0 else f
        rows = pl.ds(pl.multiple_of(h * H, H), H)
        v = product_nt(epg[0], wei[0, rows, :]) + product_nt(epg[1], wei[1, rows, :])
        out = (ge[h].astype(F32) + v.astype(BF16).astype(F32)).astype(BF16)
        if hh == 0:
            dbuf[...] = out
            send(dbuf, o_edges.at[mine], fs.at[9], fr.at[9], partner)
        else:
            o_edges[mine, :] = out
    advance(efirst + 4)
    for hh in range(2):
        h = g if hh == 0 else f
        rows_s = pl.ds(pl.multiple_of(D + h * H, H), H)
        rows_r = pl.ds(pl.multiple_of(2 * D + h * H, H), H)
        vs = (product_nt(epg[0], wei[0, rows_s, :]) + product_nt(epg[1], wei[1, rows_s, :])).astype(BF16)
        vr = (product_nt(epg[0], wei[0, rows_r, :]) + product_nt(epg[1], wei[1, rows_r, :])).astype(BF16)
        tgv = product(hot_s[...], vs)
        tg[h] = tgv[N : N + nD * SLOT].astype(BF16)
        for o in range(1, nD):
            q = lax.rem(d + o, nD)
            send(
                tg.at[h, pl.ds(pl.multiple_of(q * SLOT, SLOT), SLOT)],
                hback.at[f, pl.ds(pl.multiple_of(d * SLOT, SLOT), SLOT)],
                ts.at[q, h], tr.at[d, f], {"dom": q, "feat": h},
            )
        nv = tgv[:N] + product(hot_r[...], vr)
        advance(efirst + 6 + 2 * hh)
        if hh == 0:
            np_send[...] = nv
            send(np_send, np_recv, fs.at[10], fr.at[10], partner)
    rows = pl.ds(pl.multiple_of(f * H, H), H)
    nv += product_nt(n_pg[0], wni[0, rows, :]) + product_nt(n_pg[1], wni[1, rows, :])
    remote(np_recv, np_recv, fs.at[10], fr.at[10], partner).wait_recv()
    nv += np_recv[...]
    for o in range(1, nD):
        q = lax.rem(d + nD - o, nD)
        for h in range(2):
            dst = hback.at[h, pl.ds(pl.multiple_of(q * SLOT, SLOT), SLOT)]
            remote(dst, dst, ts.at[q, h], tr.at[q, h], partner).wait_recv()
    hot_h = jnp.where(
        lax.broadcasted_iota(jnp.int32, (N, HP), 0) == ints[:, 4 * R :], 1.0, 0.0
    ).astype(BF16)
    nv += product(hot_h, hback[0]) + product(hot_h, hback[1])
    o_nodes[...] = nv.astype(BF16)
    advance(nch + LAG_D)
    dst = o_edges.at[theirs]
    remote(dst, dst, fs.at[9], fr.at[9], partner).wait_recv()

    for cp in pending:
        cp.wait_send()
    for c in range(nch):
        @pl.when(jnp.logical_not(is_root))
        def _():
            up_copy(c).wait_send()

        @pl.when(jnp.logical_or(is_root, jnp.logical_not(leaf)))
        def _():
            down_copy(c, 0, away).wait_send()

        @pl.when(is_root)
        def _():
            down_copy(c, 1, away).wait_send()


def spread(rows, nodes, edges, dw, o_nodes, o_edges, *outs):
    o_nodes[0] = nodes[...]
    o_edges[0] = edges[...]
    at = 0
    for r, out in zip(rows, outs):
        out[...] = dw[at : at + r].astype(F32).reshape(r * CHUNK, dw.shape[2])
        at += r


def shards(node_latents, edge_latents, grad_nodes, grad_edges, edge_sender, edge_receiver,
           halo_rows, w_ei, w_eo, w_ni, w_no):
    nD, nS = lax.axis_size("dom"), lax.axis_size("dp")
    N, EC = node_latents.shape[1], edge_latents.shape[1]
    H = node_latents.shape[2]
    D = 2 * H
    R = EC // 2
    K = halo_rows.shape[2]
    HP = round_up(nD * SLOT, 128)
    Tp = round_up(N + nD * SLOT, 128)
    mul = -(-(1 << 19) // K)
    assert all((v * mul) >> 19 == v // K for v in range(nD * K))
    halo = jnp.pad(
        halo_rows[0], ((0, HP // SLOT - nD), (0, SLOT - K)), constant_values=-1
    ).reshape(-1)
    ints = jnp.concatenate([edge_sender, edge_receiver, halo]).reshape(1, -1)
    nch = 7 * D // nS // CHUNK
    nce = 4 * D // nS // CHUNK
    cfg = dict(
        nD=nD, nS=nS, N=N, R=R, HALO=K, MUL=mul,
        edge_factor=1.0 / math.sqrt(nS * EC * nD), node_factor=1.0 / math.sqrt(nS * N * nD),
    )
    vm = lambda shape, dt=BF16: pltpu.VMEM(shape, dt)
    sem = lambda *shape: pltpu.SemaphoreType.DMA(shape)
    any_, vmem = pl.BlockSpec(memory_space=pl.ANY), pl.BlockSpec(memory_space=pltpu.VMEM)
    scratch = [
        vm((2, Tp, H)), vm((2, N, H)), vm((2, R, H)), vm((2, R, H)),
        vm((2, 3 * D, H)), vm((2, D, H)), vm((2, 2 * D, H)), vm((2, D, H)),
        vm((HP, H)), vm((Tp, R)), vm((N, R)), vm((R, 3 * D)), vm((2, R, H), F32), vm((R, D)),
        vm((2, R, H), F32), vm((N, D), F32), vm((N, D), F32),
        vm((N, 2 * D)), vm((N, D)), vm((2, N, H)), vm((2, N, H)), vm((N, D)),
        vm((2, R, H)), vm((2, R, H)), vm((R, H)), vm((N, H), F32), vm((N, H), F32),
        vm((2, nD * SLOT, H)), vm((2, HP, H)),
        vm((nS, nce, CHUNK, H)), vm((nS, nce, CHUNK, H)), vm((8, 128), F32),
        vm((nS, nch, CHUNK, H)), vm((nS, nch, CHUNK, H)), vm((nch, CHUNK, H), F32),
        vm((nch, CHUNK, H)), vm((2, nch, CHUNK, H)),
        sem(8), sem(11 + 2 * nS), sem(11 + 2 * nS), sem(nD, 2), sem(nD, 2), sem(nD, 2), sem(nD, 2),
        sem(nS, nch), sem(nS, nch), sem(nch), sem(2, nch), sem(2, nch), sem(nch),
    ]
    d_nodes, d_edges, dw = pl.pallas_call(
        functools.partial(kernel, cfg),
        out_shape=(
            jax.ShapeDtypeStruct((N, H), BF16),
            jax.ShapeDtypeStruct((EC, H), BF16),
            jax.ShapeDtypeStruct((nch, CHUNK, H), BF16),
        ),
        in_specs=[any_] * 8 + [vmem],
        out_specs=(vmem, vmem, vmem),
        scratch_shapes=scratch,
        compiler_params=pltpu.CompilerParams(
            collective_id=0, has_side_effects=True, vmem_limit_bytes=62 * 1024 * 1024
        ),
        cost_estimate=pl.CostEstimate(
            flops=4_000_000_000, bytes_accessed=8_000_000, transcendentals=1_000_000
        ),
    )(node_latents, edge_latents, grad_nodes, grad_edges, w_ei, w_eo, w_ni, w_no,
      ints)
    rows = (D // nS // CHUNK, 2 * D // nS // CHUNK, D // nS // CHUNK, 3 * D // nS // CHUNK)
    out = lambda r: jax.ShapeDtypeStruct((r * CHUNK, H), F32)
    d_nodes, d_edges, g_no, g_ni, g_eo, g_ei = pl.pallas_call(
        functools.partial(spread, rows),
        out_shape=(
            jax.ShapeDtypeStruct((1, N, H), BF16), jax.ShapeDtypeStruct((1, EC, H), BF16),
            out(rows[0]), out(rows[1]), out(rows[2]), out(rows[3]),
        ),
        in_specs=[vmem] * 3,
        out_specs=(vmem,) * 6,
        compiler_params=pltpu.CompilerParams(vmem_limit_bytes=62 * 1024 * 1024),
        cost_estimate=pl.CostEstimate(flops=500_000, bytes_accessed=4_000_000, transcendentals=0),
    )(d_nodes, d_edges, dw)
    return d_nodes, d_edges, g_ei, g_eo, g_ni, g_no


def solution(mesh):
    whole = P(("group", "dp"), "dom", "feat")
    weight = P(None, "feat")
    share = P(("group", "dp"), "feat")
    return jax.shard_map(
        shards,
        mesh=mesh,
        in_specs=(whole,) * 4 + (P("dom"), P("dom"), P("dom", None, None)) + (weight,) * 4,
        out_specs=(whole, whole, share, share, share, share),
        check_vma=False,
    )
```
